256 devices in a mesh: dp: 16 (over z_lo, x), seq: 16 (over z_hi, y, core).
Axes of the slice: x: 4, y: 4, z: 8 (z_hi: 2, z_lo: 4; z = z_hi * 4 + z_lo), core: 2. Of those that a mesh axis runs over, the one named last changes fastest.
Arguments:
- query: bfloat16 [16, 2048, 1536], P('dp', 'seq'), may hold values from -10 to 10
- key_proj: bfloat16 [16, 2048, 1536], P('dp', 'seq'), may hold values from -10 to 10
- value: bfloat16 [16, 2048, 1536], P('dp', 'seq'), may hold values from -6 to 6
- cotangent: bfloat16 [16, 2048, 1536], P('dp', 'seq'), may hold values from -6 to 6
- out_weight: bfloat16 [1536, 1536], P(('dp', 'seq')), may hold values from -0.15625 to 0.15625
Outputs:
- projected: bfloat16 [16, 2048, 1536], P('dp', 'seq')
- grad_query: bfloat16 [16, 2048, 1536], P('dp', 'seq')
- grad_key: bfloat16 [16, 2048, 1536], P('dp', 'seq')
- grad_value: bfloat16 [16, 2048, 1536], P('dp', 'seq')
- grad_weight: float32 [1536, 1536], P(('dp', 'seq'))
The draws below stay inside these ranges and needn't reach their ends.
All inputs are finite; a program needn't handle non-finite values.
Results may differ from the reference program's by a relative error of at most 0.015.
Values may be sent and summed in bfloat16 or wider, within the bound.
No kernel may reach another device: no remote copies, remote signals or barrier semaphores. Data moves between devices by JAX's collectives and lax.ppermute only.
A program may use at most 128 MiB of HBM per device.

```python
import math
import jax
import jax.numpy as jnp
from jax import lax

D = 1536
H = 16
HD = 96
UTT = 16
LEN = 2048


def draw_query(key, part):
    key = jax.random.fold_in(key, 1)
    values_drawn = 3.0 * jnp.clip(jax.random.normal(key, (UTT, LEN, D), jnp.float32), -3.3, 3.3)
    return values_drawn.astype(jnp.bfloat16)


def draw_key_proj(key, part):
    key = jax.random.fold_in(key, 2)
    values_drawn = jnp.clip(jax.random.normal(key, (UTT, LEN, D), jnp.float32), -3.3, 3.3)
    return values_drawn.astype(jnp.bfloat16)


def block_levels(key, extent, split, smallest, top_value):
    gain, own = 1.0, jax.random.fold_in(key, 6)
    for dim, shards_of in split:
        heights = jnp.exp(jax.random.uniform(jax.random.fold_in(own, dim), (shards_of,), jnp.float32, smallest / len(split), top_value / len(split)))
        gain = gain * jnp.repeat(heights, extent[dim] // shards_of).reshape([-1 if axis == dim else 1 for axis in range(len(extent))])
    return gain


def centred(key, shape, deviation, most, pieces=(), kind=jnp.bfloat16):
    loudness = block_levels(key, shape, pieces, -0.22, 0.18) if pieces else 1.0
    values = jax.random.normal(key, shape, jnp.float32) * deviation * loudness
    return jnp.minimum(jnp.maximum(values, -most), most).astype(kind)


def setup_inputs(seed: int = 0) -> dict:
    key_of = jax.random.split(jax.random.key(seed), 6)
    return {
        "query": draw_query(jax.random.fold_in(key_of[5], 71), 0),
        "key_proj": draw_key_proj(jax.random.fold_in(key_of[5], 71), 0),
        "value": centred(key_of[2], (UTT, LEN, D), 1.0, 6.0, ((0, 16), (1, 16))),
        "cotangent": centred(key_of[3], (UTT, LEN, D), 1.0, 6.0, ((0, 16), (1, 16))),
        "out_weight": centred(key_of[4], (D, D), D ** -0.5, 0.15625, ((0, 256),)),
    }


def to_pairs(array_in):
    return array_in.reshape(UTT, LEN, H, HD).transpose(0, 2, 1, 3).reshape(UTT * H, LEN, HD)

def from_pairs(array_in):
    return array_in.reshape(UTT, H, LEN, HD).transpose(0, 2, 1, 3).reshape(UTT, LEN, D)

def one_head(inputs):
    q_head, k_head, v_head, g_head = inputs
    factor = 1.0 / math.sqrt(HD)
    scores = jnp.dot(q_head, k_head.T, preferred_element_type=jnp.float32) * factor
    top_score = lax.optimization_barrier(jnp.max(scores, axis=1, keepdims=True))
    exp_scores = jnp.exp(scores - top_score)
    prob_rows = exp_scores / lax.optimization_barrier(jnp.sum(exp_scores, axis=1, keepdims=True))
    prob_weights = prob_rows.astype(jnp.bfloat16)
    attended = jnp.dot(prob_weights, v_head, preferred_element_type=jnp.float32).astype(jnp.bfloat16)
    grad_probs = jnp.dot(g_head, v_head.T, preferred_element_type=jnp.float32)
    row_delta = lax.optimization_barrier(jnp.sum(grad_probs * prob_rows, axis=1, keepdims=True))
    grad_scores = (prob_rows * (grad_probs - row_delta) * factor).astype(jnp.bfloat16)
    grad_value = jnp.dot(prob_weights.T, g_head, preferred_element_type=jnp.float32).astype(jnp.bfloat16)
    grad_query = jnp.dot(grad_scores, k_head, preferred_element_type=jnp.float32).astype(jnp.bfloat16)
    grad_key = jnp.dot(grad_scores.T, q_head, preferred_element_type=jnp.float32).astype(jnp.bfloat16)
    return (attended, grad_query, grad_key, grad_value)

def reference(query, key_proj, value, cotangent, out_weight):
    grad_rows = cotangent.reshape(UTT * LEN, D)
    grad_attended = lax.dot_general(grad_rows, out_weight, (((1,), (1,)), ((), ())), preferred_element_type=jnp.float32).astype(jnp.bfloat16)
    results = lax.map(one_head, (to_pairs(query), to_pairs(key_proj), to_pairs(value), to_pairs(grad_attended.reshape(UTT, LEN, D))))
    attended_rows = from_pairs(results[0]).reshape(UTT * LEN, D)
    projected = jnp.dot(attended_rows, out_weight, preferred_element_type=jnp.float32).astype(jnp.bfloat16).reshape(UTT, LEN, D)
    grad_weight = lax.dot_general(attended_rows, grad_rows, (((0,), (0,)), ((), ())), preferred_element_type=jnp.float32)
    return (projected, from_pairs(results[1]), from_pairs(results[2]), from_pairs(results[3]), grad_weight)
```

```python
import functools
import math

import jax
import jax.numpy as jnp
from jax import lax
from jax.experimental import pallas as pl
from jax.experimental.pallas import tpu as pltpu
from jax.sharding import Mesh
from jax.sharding import PartitionSpec as P

HD = 96
FACTOR = 1.0 / math.sqrt(HD)
LOG2E = math.log2(math.e)
C2 = FACTOR * LOG2E
F32 = jnp.float32
BF16 = jnp.bfloat16
NB = 8
FB = 128
QB = 2
PAIR = 2 * HD
ALL = ("zl", "x", "zh", "y", "c")
YC = ("y", "c")
G32 = ("zl", "x", "zh")


def vmem_specs(count):
    return [pl.BlockSpec(memory_space=pltpu.VMEM) for _ in range(count)]


def call(kernel, ins, outs, scratch=(), flops=0, name=None):
    nbytes = sum(a.size * a.dtype.itemsize for a in list(ins) + list(outs))
    return pl.pallas_call(
        kernel,
        out_shape=tuple(outs),
        in_specs=vmem_specs(len(ins)),
        out_specs=tuple(vmem_specs(len(outs))),
        scratch_shapes=list(scratch),
        cost_estimate=pl.CostEstimate(flops=flops, bytes_accessed=nbytes, transcendentals=0),
        compiler_params=pltpu.CompilerParams(vmem_limit_bytes=56 * 2**20),
        name=name,
    )(*ins)


def shape(dims, dtype):
    return jax.ShapeDtypeStruct(dims, dtype)


def nn(a, b):
    return jnp.dot(a, b, preferred_element_type=F32)


def heads_of(head, offset=0):
    return slice(offset + head * HD, offset + (head + 1) * HD)


def cols(ref, step, rows):
    return jnp.concatenate([ref[step * QB + t, rows, :] for t in range(QB)], axis=1)


def put_cols(ref, step, rows, value):
    for t in range(QB):
        ref[step * QB + t, rows, :] = value[:, t * FB : (t + 1) * FB].astype(ref.dtype)


def rows_from(ref, rows, out):
    for b in range(NB):
        out[b * FB : (b + 1) * FB, :] = ref[b, rows, :].T


def wide_from(ref, rows, out):
    for b in range(NB):
        out[:, b * FB : (b + 1) * FB] = ref[b, rows, :]


def prep_kernel(count, *refs):
    out = refs[count]
    for n in range(count):
        for b in range(NB):
            out[b, n * PAIR : (n + 1) * PAIR, :] = refs[n][:, b * PAIR : (b + 1) * PAIR].T


def prep(*arrays):
    count = len(arrays)
    return call(
        functools.partial(prep_kernel, count),
        arrays,
        [shape((NB, count * PAIR, FB), BF16)],
        name="prep",
    )[0]


def fwd_kernel(second, *refs):
    if second:
        q, kv, st_in, acc_in, att, acc_out, st_out, k_s, vt_s = refs
    else:
        q, kv, acc_out, st_out, k_s, vt_s = refs
    st_out[...] = jnp.zeros_like(st_out)
    for head in range(2):
        rows = heads_of(head)
        rows_from(kv, rows, k_s)
        wide_from(kv, heads_of(head, PAIR), vt_s)

        def step(i, carry, rows=rows, head=head):
            scores = nn(k_s[...], cols(q, i, rows))
            top = jnp.max(scores, axis=0, keepdims=True) * C2
            if second:
                top_old = cols(st_in, i, slice(head, head + 1))
                top = jnp.maximum(top, top_old)
            probs = jnp.exp2(scores * C2 - top)
            total = jnp.sum(probs, axis=0, keepdims=True)
            acc = nn(vt_s[...], probs.astype(BF16))
            if second:
                alpha = jnp.exp2(top_old - top)
                total = total + alpha * cols(st_in, i, slice(2 + head, 3 + head))
                acc = acc + alpha * cols(acc_in, i, rows)
                acc = acc / total
                put_cols(att, i, rows, acc)
                put_cols(st_out, i, slice(head, head + 1), top + jnp.log2(total))
            else:
                put_cols(st_out, i, slice(head, head + 1), top)
                put_cols(st_out, i, slice(2 + head, 3 + head), total)
            put_cols(acc_out, i, rows, acc)
            return carry

        lax.fori_loop(0, NB // QB, step, 0)


def forward(q, kv, state=None):
    second = state is not None
    outs = [shape((NB, PAIR, FB), F32), shape((NB, 8, FB), F32)]
    if second:
        outs = [shape((NB, PAIR, FB), BF16)] + outs
    ins = [q, kv] + (list(state) if second else [])
    return call(
        functools.partial(fwd_kernel, second),
        ins,
        outs,
        [pltpu.VMEM((NB * FB, HD), BF16), pltpu.VMEM((HD, NB * FB), BF16)],
        flops=4 * 2 * 1024 * 1024 * 256,
        name="fwd_rem" if second else "fwd_own",
    )


def grad_kernel(w32, cot, w_out, g_out, w_s):
    for n in range(32):
        w_s[n * 6 : (n + 1) * 6, :] = w32[n].astype(F32)
    w_pair = w_s[...].astype(BF16)
    w_out[...] = w_pair
    for b in range(NB):
        g_out[b] = lax.dot_general(
            w_pair, cot[b * FB : (b + 1) * FB, :], (((1,), (1,)), ((), ())), preferred_element_type=F32
        ).astype(BF16)


def grad_attended(w32, cot):
    return call(
        grad_kernel,
        [w32, cot],
        [shape((PAIR, 1536), BF16), shape((NB, PAIR, FB), BF16)],
        [pltpu.VMEM((PAIR, 1536), F32)],
        flops=2 * 192 * 1536 * 1024,
        name="grad_att",
    )


def delta_kernel(g, acc, st_in, st_out):
    for b in range(NB):
        st_out[b] = st_in[b]
        for head in range(2):
            rows = heads_of(head)
            st_out[b, 2 + head : 3 + head, :] = jnp.sum(
                g[b, rows, :].astype(F32) * acc[b, rows, :], axis=0, keepdims=True
            )


def deltas(g, acc, stats):
    return call(delta_kernel, [g, acc, stats], [shape((NB, 8, FB), F32)], name="delta")[0]


def bwd_kernel(need_q, need_k, first, last, *refs):
    refs = list(refs)
    q, g, st, kv = refs[:4]
    del refs[:4]
    dq_in = dkv_in = None
    if need_q and not first:
        dq_in = refs.pop(0)
    if need_k and not first:
        dk_in, dv_in = refs.pop(0), refs.pop(0)
    dq = refs.pop(0) if need_q else None
    if need_k:
        if last:
            dkv = refs.pop(0)
        else:
            dk_out, dv_out = refs.pop(0), refs.pop(0)
    k_s, v_s = refs.pop(0), refs.pop(0)
    if need_q:
        kt_s = refs.pop(0)
    if need_k:
        q_s, g_s, dk_s, dv_s = refs
    for head in range(2):
        rows = heads_of(head)
        rows_from(kv, rows, k_s)
        rows_from(kv, heads_of(head, PAIR), v_s)
        if need_q:
            wide_from(kv, rows, kt_s)
        if need_k:
            rows_from(q, rows, q_s)
            rows_from(g, rows, g_s)
            if first:
                dk_s[...] = jnp.zeros_like(dk_s)
                dv_s[...] = jnp.zeros_like(dv_s)
            else:
                dk_s[...] = dk_in[head]
                dv_s[...] = dv_in[head]

        def step(i, carry, rows=rows, head=head):
            lse = cols(st, i, slice(head, head + 1))
            delta = cols(st, i, slice(2 + head, 3 + head))
            scores = nn(k_s[...], cols(q, i, rows))
            probs = jnp.exp2(scores * C2 - lse)
            gprobs = nn(v_s[...], cols(g, i, rows))
            ds = (probs * (gprobs - delta)).astype(BF16)
            if need_q:
                acc = nn(kt_s[...], ds)
                if dq_in is not None:
                    acc = acc + cols(dq_in, i, rows)
                if last:
                    acc = acc * FACTOR
                put_cols(dq, i, rows, acc)
            if need_k:
                at = pl.ds(pl.multiple_of(i * (QB * FB), QB * FB), QB * FB)
                dv_s[...] += nn(probs.astype(BF16), g_s[at, :])
                dk_s[...] += nn(ds, q_s[at, :])
            return carry

        lax.fori_loop(0, NB // QB, step, 0)
        if need_k:
            if last:
                for b in range(NB):
                    part = slice(b * FB, (b + 1) * FB)
                    dkv[b, rows, :] = (dk_s[part, :] * FACTOR).T.astype(BF16)
                    dkv[b, heads_of(head, PAIR), :] = dv_s[part, :].T.astype(BF16)
            else:
                dk_out[head] = dk_s[...]
                dv_out[head] = dv_s[...]


def backward(q, g, stats, kv, dq=None, dkv=None, need_q=False, need_k=False, first=False, last=False, name=None):
    ins = [q, g, stats, kv]
    if dq is not None:
        ins.append(dq)
    if dkv is not None:
        ins += list(dkv)
    outs = []
    if need_q:
        outs.append(shape((NB, PAIR, FB), BF16 if last else F32))
    if need_k:
        if last:
            outs.append(shape((NB, 2 * PAIR, FB), BF16))
        else:
            outs += [shape((2, NB * FB, HD), F32)] * 2
    tall = pltpu.VMEM((NB * FB, HD), BF16)
    scratch = [tall, tall]
    if need_q:
        scratch.append(pltpu.VMEM((HD, NB * FB), BF16))
    if need_k:
        scratch += [tall, tall, pltpu.VMEM((NB * FB, HD), F32), pltpu.VMEM((NB * FB, HD), F32)]
    products = 2 + need_q + 2 * need_k
    return call(
        functools.partial(bwd_kernel, need_q, need_k, first, last),
        ins,
        outs,
        scratch,
        flops=products * 2 * 2 * 1024 * 1024 * 256,
        name=name,
    )


def weight_kernel(att, cot, out, w_s):
    acc = jnp.zeros((PAIR, 1536), F32)
    for b in range(NB):
        acc = acc + nn(att[b], cot[b * FB : (b + 1) * FB, :])
    w_s[...] = acc
    for n in range(32):
        out[n] = w_s[n * 6 : (n + 1) * 6, :].astype(BF16)


def weight_part(att, cot):
    return call(
        weight_kernel,
        [att, cot],
        [shape((32, 6, 1536), BF16)],
        [pltpu.VMEM((PAIR, 1536), F32)],
        flops=2 * 192 * 1536 * 1024,
        name="grad_w",
    )[0]


def back_kernel(count, src, *outs):
    for n in range(count):
        for b in range(NB):
            outs[n][:, b * PAIR : (b + 1) * PAIR] = src[b, n * PAIR : (n + 1) * PAIR, :].T


def back(src):
    count = src.shape[1] // PAIR
    return call(
        functools.partial(back_kernel, count), [src], [shape((FB, 1536), BF16)] * count, name="back"
    )


def weight_pairs():
    pairs = []
    for a in range(8):
        for n in range(32):
            b, s = divmod(n, 16)
            pairs.append(((2 * a + b) * 16 + s, n * 8 + a))
    return pairs


def body(query, key_proj, value, cotangent, out_weight):
    flip = [(0, 1), (1, 0)]
    a2a = functools.partial(lax.all_to_all, split_axis=0, concat_axis=0, tiled=True)
    swap = lambda x: lax.ppermute(x, "zh", flip)

    kv = a2a(prep(key_proj[0], value[0]), YC)
    q = a2a(prep(query[0]), YC)
    w_mine = lax.ppermute(out_weight, ALL, weight_pairs())
    w32 = a2a(jnp.broadcast_to(w_mine[None], (32, 6, 1536)), G32)
    cot = lax.all_gather(cotangent[0], YC, axis=0, tiled=True)
    kv_far = swap(kv)
    q_far = swap(q)

    state = forward(q, kv)
    w_pair, g = grad_attended(w32, cot)
    g_far = swap(g)
    w_full = lax.all_gather(w_pair, YC, axis=0, tiled=True)
    att, acc, stats = forward(q, kv_far, state=(state[1], state[0]))
    att_rows = a2a(att, YC).reshape(1536, FB)
    stats = deltas(g, acc, stats)
    stats_far = swap(stats)
    dq, dk, dv = backward(q, g, stats, kv, need_q=True, need_k=True, first=True, name="bwd_own")
    (dq,) = backward(q, g, stats, kv_far, dq=dq, need_q=True, last=True, name="bwd_q")
    dq_rows = a2a(dq, YC)
    (dkv,) = backward(q_far, g_far, stats_far, kv, dkv=(dk, dv), need_k=True, last=True, name="bwd_k")
    dkv_rows = a2a(dkv, YC)

    parts = a2a(weight_part(att, cot), G32)
    grad_weight = jnp.sum(parts.astype(F32), axis=0)
    grad_weight = lax.ppermute(grad_weight, ALL, [(d, s) for s, d in weight_pairs()])

    projected = lax.dot_general(
        att_rows, w_full, (((0,), (0,)), ((), ())), preferred_element_type=F32
    ).astype(BF16)
    (grad_query,) = back(dq_rows)
    grad_key, grad_value = back(dkv_rows)
    return (projected[None], grad_query[None], grad_key[None], grad_value[None], grad_weight)


def solution(mesh):
    fine = Mesh(mesh.devices.reshape(4, 4, 2, 4, 2), ALL)
    rows = P(("zl", "x"), ("zh", "y", "c"), None)
    weight = P(ALL, None)
    return jax.shard_map(
        body,
        mesh=fine,
        in_specs=(rows, rows, rows, rows, weight),
        out_specs=(rows, rows, rows, rows, weight),
        check_vma=False,
    )
```

```python
import functools
import math

import jax
import jax.numpy as jnp
from jax import lax
from jax.experimental import pallas as pl
from jax.experimental.pallas import tpu as pltpu
from jax.sharding import Mesh
from jax.sharding import PartitionSpec as P

HD = 96
FACTOR = 1.0 / math.sqrt(HD)
LOG2E = math.log2(math.e)
C2 = FACTOR * LOG2E
F32 = jnp.float32
BF16 = jnp.bfloat16
NB = 16
HALF = 8
FB = 128
QB = 2
FRAMES = NB * FB
PAIR = 2 * HD
WIDTH = NB * HD
ALL = ("zl", "x", "zh", "y", "c")
SEQ = ("zh", "y", "c")
YC = ("y", "c")
Z8 = ("zl", "zh")


def call(kernel, ins, outs, scratch=(), side=False, us=1, name=None):
    vmem = pl.BlockSpec(memory_space=pltpu.VMEM)
    specs = [vmem for _ in ins]
    if side:
        ins = list(ins) + [lax.axis_index("zh").astype(jnp.int32).reshape(1)]
        specs.append(pl.BlockSpec(memory_space=pltpu.SMEM))
    return pl.pallas_call(
        kernel,
        out_shape=tuple(outs),
        in_specs=specs,
        out_specs=tuple(vmem for _ in outs),
        scratch_shapes=list(scratch),
        cost_estimate=pl.CostEstimate(flops=int(us * 1.1e9), bytes_accessed=1, transcendentals=0),
        compiler_params=pltpu.CompilerParams(vmem_limit_bytes=56 * 2**20),
        name=name,
    )(*ins)


def shape(dims, dtype):
    return jax.ShapeDtypeStruct(dims, dtype)


def nn(a, b):
    return jnp.dot(a, b, preferred_element_type=F32)


Q, K, V = (slice(n * HD, (n + 1) * HD) for n in range(3))
ANY = slice(0, HD)


def cols(ref, step, rows):
    return jnp.concatenate([ref[step * QB + t, rows, :] for t in range(QB)], axis=1)


def put_cols(ref, step, rows, value):
    for t in range(QB):
        ref[step * QB + t, rows, :] = value[:, t * FB : (t + 1) * FB].astype(ref.dtype)


def rows_from(ref, rows, out):
    for b in range(NB):
        out[b * FB : (b + 1) * FB, :] = ref[b, rows, :].T


def wide_from(ref, rows, out):
    for b in range(NB):
        out[:, b * FB : (b + 1) * FB] = ref[b, rows, :]


def prep_kernel(q, k, v, out):
    for n, ref in enumerate((q, k, v)):
        for part in range(4):
            four = ref[:, part * 4 * HD : (part + 1) * 4 * HD].T
            for h in range(4):
                out[part * 4 + h, n * HD : (n + 1) * HD, :] = four[h * HD : (h + 1) * HD, :]


def prep(q, k, v):
    return call(prep_kernel, [q, k, v], [shape((NB, 3 * HD, FB), BF16)], us=2.6, name="prep")[0]


def back_kernel(src, *outs):
    for n, out in enumerate(outs):
        for part in range(4):
            four = [src[part * 4 + h, n * HD : (n + 1) * HD, :] for h in range(4)]
            out[:, part * 4 * HD : (part + 1) * 4 * HD] = jnp.concatenate(four, axis=0).T


def back(src):
    return call(back_kernel, [src], [shape((FB, WIDTH), BF16)] * 3, us=2.4, name="back")


def fwd_kernel(qkv, side, keep, send, acc_out, lse_out, k_s, vt_s, att):
    rows_from(qkv, K, k_s)
    wide_from(qkv, V, vt_s)
    lse_out[...] = jnp.zeros_like(lse_out)

    def step(i, carry):
        scores = nn(k_s[...], cols(qkv, i, Q))
        top = jnp.max(scores, axis=0, keepdims=True) * C2
        probs = jnp.exp2(scores * C2 - top)
        total = jnp.sum(probs, axis=0, keepdims=True)
        acc = nn(vt_s[...], probs.astype(BF16)) / total
        put_cols(att, i, ANY, acc)
        put_cols(acc_out, i, ANY, acc)
        put_cols(lse_out, i, slice(0, 1), top + jnp.log2(total))
        return carry

    lax.fori_loop(0, NB // QB, step, 0)
    mine = side[0] * HALF
    for b in range(HALF):
        keep[b] = att[mine + b]
        send[b] = att[HALF - mine + b]


def forward(qkv):
    half = shape((HALF, HD, FB), BF16)
    return call(
        fwd_kernel,
        [qkv],
        [half, half, shape((NB, HD, FB), F32), shape((NB, 8, FB), F32)],
        [
            pltpu.VMEM((FRAMES, HD), BF16),
            pltpu.VMEM((HD, FRAMES), BF16),
            pltpu.VMEM((NB, HD, FB), BF16),
        ],
        side=True,
        us=12.4,
        name="fwd",
    )


def grad_kernel(w32, cot, att, side, keep, send, proj, w_s):
    for n in range(32):
        w_s[n * 6 : (n + 1) * 6, :] = w32[n].astype(F32)
    w_pair = w_s[...].astype(BF16)
    low = side[0] == 0
    for b in range(HALF):
        rows = slice(b * FB, (b + 1) * FB)
        both = lax.dot_general(
            w_pair, cot[rows, :], (((1,), (1,)), ((), ())), preferred_element_type=F32
        )
        keep[b] = jnp.where(low, both[:HD], both[HD:]).astype(BF16)
        send[b] = jnp.where(low, both[HD:], both[:HD]).astype(BF16)
        proj[rows, :] = nn(att[b].T, w_pair).astype(BF16)


def grad_attended(w32, cot, att_pair):
    half = shape((HALF, HD, FB), BF16)
    return call(
        grad_kernel,
        [w32, cot, att_pair],
        [half, half, shape((HALF * FB, WIDTH), BF16)],
        [pltpu.VMEM((PAIR, WIDTH), F32)],
        side=True,
        us=6.1,
        name="grad_att",
    )


def bwd_kernel(qkv, keep, recv, acc_in, lse_in, side, out, k_s, v_s, kt_s, q_s, g_s, gt_s, dk_s, dv_s):
    mine = side[0] * HALF
    for b in range(HALF):
        gt_s[mine + b] = keep[b]
        gt_s[HALF - mine + b] = recv[b]
    rows_from(qkv, K, k_s)
    rows_from(qkv, V, v_s)
    rows_from(qkv, Q, q_s)
    rows_from(gt_s, ANY, g_s)
    wide_from(qkv, K, kt_s)
    dk_s[...] = jnp.zeros_like(dk_s)
    dv_s[...] = jnp.zeros_like(dv_s)

    def step(i, carry):
        g = cols(gt_s, i, ANY)
        delta = jnp.sum(g.astype(F32) * cols(acc_in, i, ANY), axis=0, keepdims=True)
        scores = nn(k_s[...], cols(qkv, i, Q))
        probs = jnp.exp2(scores * C2 - cols(lse_in, i, slice(0, 1)))
        gprobs = nn(v_s[...], g)
        ds = (probs * (gprobs - delta)).astype(BF16)
        put_cols(out, i, Q, nn(kt_s[...], ds) * FACTOR)
        at = pl.ds(pl.multiple_of(i * (QB * FB), QB * FB), QB * FB)
        dv_s[...] += nn(probs.astype(BF16), g_s[at, :])
        dk_s[...] += nn(ds, q_s[at, :])
        return carry

    lax.fori_loop(0, NB // QB, step, 0)
    for b in range(NB):
        part = slice(b * FB, (b + 1) * FB)
        out[b, K, :] = (dk_s[part, :] * FACTOR).T.astype(BF16)
        out[b, V, :] = dv_s[part, :].T.astype(BF16)


def backward(qkv, keep, recv, acc, lse):
    tall = pltpu.VMEM((FRAMES, HD), BF16)
    total = pltpu.VMEM((FRAMES, HD), F32)
    return call(
        bwd_kernel,
        [qkv, keep, recv, acc, lse],
        [shape((NB, 3 * HD, FB), BF16)],
        [
            tall,
            tall,
            pltpu.VMEM((HD, FRAMES), BF16),
            tall,
            tall,
            pltpu.VMEM((NB, HD, FB), BF16),
            total,
            total,
        ],
        side=True,
        us=16.2,
        name="bwd",
    )[0]


def weight_kernel(keep, recv, cot, side, out, pair, w_s):
    low = side[0] == 0
    acc = jnp.zeros((PAIR, WIDTH), F32)
    for b in range(HALF):
        mine, other = keep[b], recv[b]
        both = jnp.concatenate([jnp.where(low, mine, other), jnp.where(low, other, mine)], axis=0)
        pair[b] = both
        acc = acc + nn(both, cot[b * FB : (b + 1) * FB, :])
    w_s[...] = acc
    for n in range(32):
        out[n] = w_s[n * 6 : (n + 1) * 6, :].astype(BF16)


def weight_part(keep, recv, cot):
    return call(
        weight_kernel,
        [keep, recv, cot],
        [shape((32, 6, WIDTH), BF16), shape((HALF, PAIR, FB), BF16)],
        [pltpu.VMEM((PAIR, WIDTH), F32)],
        side=True,
        us=4.4,
        name="grad_w",
    )


def weight_pairs():
    pairs = []
    for a in range(8):
        for n in range(32):
            b, s = divmod(n, 16)
            x, zl, zh = n // 8, n % 8 // 2, n % 2
            pairs.append(((a + 8 * b) * 16 + s, ((zl * 4 + x) * 2 + zh) * 8 + a))
    return pairs


def body(query, key_proj, value, cotangent, out_weight):
    flip = [(0, 1), (1, 0)]
    a2a = functools.partial(lax.all_to_all, split_axis=0, concat_axis=0, tiled=True)
    swap = lambda x: lax.ppermute(x, "zh", flip)
    after = lambda x, *others: lax.optimization_barrier((x, *others))[0]

    qkv = a2a(prep(query[0], key_proj[0], value[0]), SEQ)
    w_mine = lax.ppermute(after(out_weight, qkv), ALL, weight_pairs())
    cot = lax.all_gather(after(cotangent[0], qkv), YC, axis=0, tiled=True)
    att_keep, att_send, acc, lse = forward(qkv)
    att_recv = swap(att_send)
    w8 = a2a(after(jnp.broadcast_to(w_mine[None], (8, 6, WIDTH)), lse), Z8)
    w8 = after(w8, att_recv)
    w32 = a2a(jnp.broadcast_to(w8[None], (4, 8, 6, WIDTH)), "x").reshape(32, 6, WIDTH)
    part, att_pair = weight_part(att_keep, att_recv, cot)
    g_keep, g_send, proj = grad_attended(after(w32, part), cot, att_pair)
    parts = a2a(part.reshape(4, 8, 6, WIDTH), "x")
    parts = jnp.sum(parts.astype(F32), axis=0).astype(BF16)
    g_recv = swap(after(g_send, parts))
    projected = lax.psum_scatter(proj, YC, scatter_dimension=0, tiled=True)
    out = backward(qkv, g_keep, g_recv, acc, after(lse, parts))
    parts = a2a(parts, Z8)
    grads = a2a(after(out, parts), SEQ)

    grad_weight = jnp.sum(parts.astype(F32), axis=0)
    grad_weight = lax.ppermute(after(grad_weight, grads), ALL, [(d, s) for s, d in weight_pairs()])
    grad_query, grad_key, grad_value = back(grads)
    return (projected[None], grad_query[None], grad_key[None], grad_value[None], grad_weight)


def solution(mesh):
    fine = Mesh(mesh.devices.reshape(4, 4, 2, 4, 2), ALL)
    rows = P(("zl", "x"), ("zh", "y", "c"), None)
    weight = P(ALL, None)
    return jax.shard_map(
        body,
        mesh=fine,
        in_specs=(rows, rows, rows, rows, weight),
        out_specs=(rows, rows, rows, rows, weight),
        check_vma=False,
    )
```

```python
import functools
import math

import jax
import jax.numpy as jnp
from jax import lax
from jax.experimental import pallas as pl
from jax.experimental.pallas import tpu as pltpu
from jax.sharding import Mesh
from jax.sharding import PartitionSpec as P

HD = 96
FACTOR = 1.0 / math.sqrt(HD)
LOG2E = math.log2(math.e)
C2 = FACTOR * LOG2E
F32 = jnp.float32
BF16 = jnp.bfloat16
NB = 16
HALF = 8
FB = 128
QB = 2
FRAMES = NB * FB
PAIR = 2 * HD
WIDTH = NB * HD
ALL = ("zl", "x", "zh", "y", "c")
SEQ = ("zh", "y", "c")
YC = ("y", "c")
Z8 = ("zl", "zh")


def call(kernel, ins, outs, scratch=(), side=False, us=1, name=None):
    vmem = pl.BlockSpec(memory_space=pltpu.VMEM)
    specs = [vmem for _ in ins]
    if side:
        ins = list(ins) + [lax.axis_index("zh").astype(jnp.int32).reshape(1)]
        specs.append(pl.BlockSpec(memory_space=pltpu.SMEM))
    return pl.pallas_call(
        kernel,
        out_shape=tuple(outs),
        in_specs=specs,
        out_specs=tuple(vmem for _ in outs),
        scratch_shapes=list(scratch),
        cost_estimate=pl.CostEstimate(flops=1, bytes_accessed=1, transcendentals=0),
        compiler_params=pltpu.CompilerParams(vmem_limit_bytes=56 * 2**20),
        name=name,
    )(*ins)


def shape(dims, dtype):
    return jax.ShapeDtypeStruct(dims, dtype)


def nn(a, b):
    return jnp.dot(a, b, preferred_element_type=F32)


Q, K, V = (slice(n * HD, (n + 1) * HD) for n in range(3))
ANY = slice(0, HD)


def cols(ref, step, rows):
    return jnp.concatenate([ref[step * QB + t, rows, :] for t in range(QB)], axis=1)


def put_cols(ref, step, rows, value):
    for t in range(QB):
        ref[step * QB + t, rows, :] = value[:, t * FB : (t + 1) * FB].astype(ref.dtype)


def rows_from(ref, rows, out):
    for b in range(NB):
        out[b * FB : (b + 1) * FB, :] = ref[b, rows, :].T


def wide_from(ref, rows, out):
    for b in range(NB):
        out[:, b * FB : (b + 1) * FB] = ref[b, rows, :]


def prep_kernel(q, k, v, out):
    for n, ref in enumerate((q, k, v)):
        for part in range(4):
            four = ref[:, part * 4 * HD : (part + 1) * 4 * HD].T
            for h in range(4):
                out[part * 4 + h, n * HD : (n + 1) * HD, :] = four[h * HD : (h + 1) * HD, :]


def prep(q, k, v):
    return call(prep_kernel, [q, k, v], [shape((NB, 3 * HD, FB), BF16)], us=2.6, name="prep")[0]


def back_kernel(src, *outs):
    for n, out in enumerate(outs):
        for part in range(4):
            four = [src[part * 4 + h, n * HD : (n + 1) * HD, :] for h in range(4)]
            out[:, part * 4 * HD : (part + 1) * 4 * HD] = jnp.concatenate(four, axis=0).T


def back(src):
    return call(back_kernel, [src], [shape((FB, WIDTH), BF16)] * 3, us=2.4, name="back")


def fwd_kernel(qkv, side, keep, send, acc_out, lse_out, k_s, vt_s, att):
    rows_from(qkv, K, k_s)
    wide_from(qkv, V, vt_s)
    lse_out[...] = jnp.zeros_like(lse_out)

    def step(i, carry):
        scores = nn(k_s[...], cols(qkv, i, Q))
        top = jnp.max(scores, axis=0, keepdims=True) * C2
        probs = jnp.exp2(scores * C2 - top)
        total = jnp.sum(probs, axis=0, keepdims=True)
        acc = nn(vt_s[...], probs.astype(BF16)) / total
        put_cols(att, i, ANY, acc)
        put_cols(acc_out, i, ANY, acc)
        put_cols(lse_out, i, slice(0, 1), top + jnp.log2(total))
        return carry

    lax.fori_loop(0, NB // QB, step, 0)
    mine = side[0] * HALF
    for b in range(HALF):
        keep[b] = att[mine + b]
        send[b] = att[HALF - mine + b]


def forward(qkv):
    half = shape((HALF, HD, FB), BF16)
    return call(
        fwd_kernel,
        [qkv],
        [half, half, shape((NB, HD, FB), F32), shape((NB, 8, FB), F32)],
        [
            pltpu.VMEM((FRAMES, HD), BF16),
            pltpu.VMEM((HD, FRAMES), BF16),
            pltpu.VMEM((NB, HD, FB), BF16),
        ],
        side=True,
        us=12.4,
        name="fwd",
    )


def grad_kernel(w32, cot, side, w_out, keep, send, w_s):
    for n in range(32):
        w_s[n * 6 : (n + 1) * 6, :] = w32[n].astype(F32)
    w_pair = w_s[...].astype(BF16)
    w_out[...] = w_pair
    low = side[0] == 0
    for b in range(HALF):
        both = lax.dot_general(
            w_pair, cot[b * FB : (b + 1) * FB, :], (((1,), (1,)), ((), ())), preferred_element_type=F32
        )
        keep[b] = jnp.where(low, both[:HD], both[HD:]).astype(BF16)
        send[b] = jnp.where(low, both[HD:], both[:HD]).astype(BF16)


def grad_attended(w32, cot):
    half = shape((HALF, HD, FB), BF16)
    return call(
        grad_kernel,
        [w32, cot],
        [shape((PAIR, WIDTH), BF16), half, half],
        [pltpu.VMEM((PAIR, WIDTH), F32)],
        side=True,
        us=4.4,
        name="grad_att",
    )


def bwd_kernel(qkv, keep, recv, acc_in, lse_in, side, out, k_s, v_s, kt_s, q_s, g_s, gt_s, dk_s, dv_s):
    mine = side[0] * HALF
    for b in range(HALF):
        gt_s[mine + b] = keep[b]
        gt_s[HALF - mine + b] = recv[b]
    rows_from(qkv, K, k_s)
    rows_from(qkv, V, v_s)
    rows_from(qkv, Q, q_s)
    rows_from(gt_s, ANY, g_s)
    wide_from(qkv, K, kt_s)
    dk_s[...] = jnp.zeros_like(dk_s)
    dv_s[...] = jnp.zeros_like(dv_s)

    def step(i, carry):
        g = cols(gt_s, i, ANY)
        delta = jnp.sum(g.astype(F32) * cols(acc_in, i, ANY), axis=0, keepdims=True)
        scores = nn(k_s[...], cols(qkv, i, Q))
        probs = jnp.exp2(scores * C2 - cols(lse_in, i, slice(0, 1)))
        gprobs = nn(v_s[...], g)
        ds = (probs * (gprobs - delta)).astype(BF16)
        put_cols(out, i, Q, nn(kt_s[...], ds) * FACTOR)
        at = pl.ds(pl.multiple_of(i * (QB * FB), QB * FB), QB * FB)
        dv_s[...] += nn(probs.astype(BF16), g_s[at, :])
        dk_s[...] += nn(ds, q_s[at, :])
        return carry

    lax.fori_loop(0, NB // QB, step, 0)
    for b in range(NB):
        part = slice(b * FB, (b + 1) * FB)
        out[b, K, :] = (dk_s[part, :] * FACTOR).T.astype(BF16)
        out[b, V, :] = dv_s[part, :].T.astype(BF16)


def backward(qkv, keep, recv, acc, lse):
    tall = pltpu.VMEM((FRAMES, HD), BF16)
    total = pltpu.VMEM((FRAMES, HD), F32)
    return call(
        bwd_kernel,
        [qkv, keep, recv, acc, lse],
        [shape((NB, 3 * HD, FB), BF16)],
        [
            tall,
            tall,
            pltpu.VMEM((HD, FRAMES), BF16),
            tall,
            tall,
            pltpu.VMEM((NB, HD, FB), BF16),
            total,
            total,
        ],
        side=True,
        us=16.2,
        name="bwd",
    )[0]


def weight_kernel(keep, recv, cot, w_pair, side, out, proj):
    low = side[0] == 0
    acc = jnp.zeros((PAIR, WIDTH), F32)
    for b in range(HALF):
        mine, other = keep[b], recv[b]
        rows = slice(b * FB, (b + 1) * FB)
        both = jnp.concatenate([jnp.where(low, mine, other), jnp.where(low, other, mine)], axis=0)
        acc = acc + nn(both, cot[rows, :])
        proj[rows, :] = nn(both.T, w_pair[...]).astype(BF16)
    out[...] = acc


def weight_part(keep, recv, cot, w_pair):
    return call(
        weight_kernel,
        [keep, recv, cot, w_pair],
        [shape((PAIR, WIDTH), F32), shape((HALF * FB, WIDTH), BF16)],
        side=True,
        us=6.4,
        name="grad_w",
    )


def weight_pairs():
    pairs = []
    for a in range(8):
        for n in range(32):
            b, s = divmod(n, 16)
            x, zl, zh = n // 8, n % 8 // 2, n % 2
            pairs.append(((a + 8 * b) * 16 + s, ((zl * 4 + x) * 2 + zh) * 8 + a))
    return pairs


def body(query, key_proj, value, cotangent, out_weight):
    flip = [(0, 1), (1, 0)]
    a2a = functools.partial(lax.all_to_all, split_axis=0, concat_axis=0, tiled=True)
    swap = lambda x: lax.ppermute(x, "zh", flip)
    after = lambda x, *others: lax.optimization_barrier((x, *others))[0]

    qkv = a2a(prep(query[0], key_proj[0], value[0]), SEQ)
    w_mine = lax.ppermute(after(out_weight, qkv), ALL, weight_pairs())
    cot = lax.all_gather(after(cotangent[0], qkv), YC, axis=0, tiled=True)
    att_keep, att_send, acc, lse = forward(qkv)
    w8 = a2a(after(jnp.broadcast_to(w_mine[None], (8, 6, WIDTH)), lse), Z8)
    att_recv = swap(att_send)
    w8 = after(w8, lse)
    w32 = a2a(jnp.broadcast_to(w8[None], (4, 8, 6, WIDTH)), "x").reshape(32, 6, WIDTH)
    w_pair, g_keep, g_send = grad_attended(w32, cot)
    g_recv = swap(after(g_send, att_recv))
    part, proj = weight_part(att_keep, att_recv, cot, w_pair)
    part = lax.psum_scatter(after(part, g_recv), "x", scatter_dimension=0, tiled=True)
    out = backward(qkv, g_keep, g_recv, acc, after(lse, proj))
    projected = lax.psum_scatter(after(proj, out), YC, scatter_dimension=0, tiled=True)
    grads = a2a(out, SEQ)
    parts = a2a(after(part, grads).astype(BF16).reshape(8, 6, WIDTH), Z8)
    grad_weight = jnp.sum(parts.astype(F32), axis=0)
    grad_weight = lax.ppermute(grad_weight, ALL, [(d, s) for s, d in weight_pairs()])

    grad_query, grad_key, grad_value = back(grads)
    return (projected[None], grad_query[None], grad_key[None], grad_value[None], grad_weight)


def solution(mesh):
    fine = Mesh(mesh.devices.reshape(4, 4, 2, 4, 2), ALL)
    rows = P(("zl", "x"), ("zh", "y", "c"), None)
    weight = P(ALL, None)
    return jax.shard_map(
        body,
        mesh=fine,
        in_specs=(rows, rows, rows, rows, weight),
        out_specs=(rows, rows, rows, rows, weight),
        check_vma=False,
    )
```

```python
import functools
import math

import jax
import jax.numpy as jnp
from jax import lax
from jax.experimental import pallas as pl
from jax.experimental.pallas import tpu as pltpu
from jax.sharding import Mesh
from jax.sharding import PartitionSpec as P

HD = 96
FACTOR = 1.0 / math.sqrt(HD)
LOG2E = math.log2(math.e)
C2 = FACTOR * LOG2E
F32 = jnp.float32
BF16 = jnp.bfloat16
NB = 16
HALF = 8
FB = 128
QB = 8
FRAMES = NB * FB
PAIR = 2 * HD
WIDTH = NB * HD
ALL = ("zl", "x", "zh", "y", "c")
SEQ = ("zh", "y", "c")
YC = ("y", "c")
Z8 = ("zl", "zh")


def call(kernel, ins, outs, scratch=(), side=False, us=1, name=None):
    vmem = pl.BlockSpec(memory_space=pltpu.VMEM)
    specs = [vmem for _ in ins]
    if side:
        ins = list(ins) + [lax.axis_index("zh").astype(jnp.int32).reshape(1)]
        specs.append(pl.BlockSpec(memory_space=pltpu.SMEM))
    return pl.pallas_call(
        kernel,
        out_shape=tuple(outs),
        in_specs=specs,
        out_specs=tuple(vmem for _ in outs),
        scratch_shapes=list(scratch),
        cost_estimate=pl.CostEstimate(flops=1, bytes_accessed=1, transcendentals=0),
        compiler_params=pltpu.CompilerParams(vmem_limit_bytes=56 * 2**20),
        name=name,
    )(*ins)


def shape(dims, dtype):
    return jax.ShapeDtypeStruct(dims, dtype)


def nn(a, b):
    return jnp.dot(a, b, preferred_element_type=F32)


Q, K, V = (slice(n * HD, (n + 1) * HD) for n in range(3))
ANY = slice(0, HD)


def cols(ref, step, rows):
    return jnp.concatenate([ref[step * QB + t, rows, :] for t in range(QB)], axis=1)


def put_cols(ref, step, rows, value):
    for t in range(QB):
        ref[step * QB + t, rows, :] = value[:, t * FB : (t + 1) * FB].astype(ref.dtype)


def rows_from(ref, rows, out):
    for b in range(NB):
        out[b * FB : (b + 1) * FB, :] = ref[b, rows, :].T


def wide_from(ref, rows, out):
    for b in range(NB):
        out[:, b * FB : (b + 1) * FB] = ref[b, rows, :]


def prep_kernel(q, k, v, out):
    for n, ref in enumerate((q, k, v)):
        for part in range(4):
            four = ref[:, part * 4 * HD : (part + 1) * 4 * HD].T
            for h in range(4):
                out[part * 4 + h, n * HD : (n + 1) * HD, :] = four[h * HD : (h + 1) * HD, :]


def prep(q, k, v):
    return call(prep_kernel, [q, k, v], [shape((NB, 3 * HD, FB), BF16)], us=2.6, name="prep")[0]


def back_kernel(src, *outs):
    for n, out in enumerate(outs):
        for part in range(4):
            four = [src[part * 4 + h, n * HD : (n + 1) * HD, :] for h in range(4)]
            out[:, part * 4 * HD : (part + 1) * 4 * HD] = jnp.concatenate(four, axis=0).T


def back(src):
    return call(back_kernel, [src], [shape((FB, WIDTH), BF16)] * 3, us=2.4, name="back")


def fwd_kernel(qkv, side, keep, send, acc_out, lse_out, k_s, vt_s, att):
    rows_from(qkv, K, k_s)
    wide_from(qkv, V, vt_s)
    lse_out[...] = jnp.zeros_like(lse_out)

    def step(i, carry):
        scores = nn(k_s[...], cols(qkv, i, Q))
        top = jnp.max(scores, axis=0, keepdims=True) * C2
        probs = jnp.exp2(scores * C2 - top)
        total = jnp.sum(probs, axis=0, keepdims=True)
        acc = nn(vt_s[...], probs.astype(BF16)) / total
        put_cols(att, i, ANY, acc)
        put_cols(acc_out, i, ANY, acc)
        put_cols(lse_out, i, slice(0, 1), top + jnp.log2(total))
        return carry

    lax.fori_loop(0, NB // QB, step, 0)
    mine = side[0] * HALF
    for b in range(HALF):
        keep[b] = att[mine + b]
        send[b] = att[HALF - mine + b]


def forward(qkv):
    half = shape((HALF, HD, FB), BF16)
    return call(
        fwd_kernel,
        [qkv],
        [half, half, shape((NB, HD, FB), F32), shape((NB, 8, FB), F32)],
        [
            pltpu.VMEM((FRAMES, HD), BF16),
            pltpu.VMEM((HD, FRAMES), BF16),
            pltpu.VMEM((NB, HD, FB), BF16),
        ],
        side=True,
        us=12.4,
        name="fwd",
    )


def grad_kernel(w32, cot, side, w_out, keep, send, w_s):
    for n in range(32):
        w_s[n * 6 : (n + 1) * 6, :] = w32[n].astype(F32)
    w_pair = w_s[...].astype(BF16)
    w_out[...] = w_pair
    low = side[0] == 0
    for b in range(HALF):
        both = lax.dot_general(
            w_pair, cot[b * FB : (b + 1) * FB, :], (((1,), (1,)), ((), ())), preferred_element_type=F32
        )
        keep[b] = jnp.where(low, both[:HD], both[HD:]).astype(BF16)
        send[b] = jnp.where(low, both[HD:], both[:HD]).astype(BF16)


def grad_attended(w32, cot):
    half = shape((HALF, HD, FB), BF16)
    return call(
        grad_kernel,
        [w32, cot],
        [shape((PAIR, WIDTH), BF16), half, half],
        [pltpu.VMEM((PAIR, WIDTH), F32)],
        side=True,
        us=4.4,
        name="grad_att",
    )


def bwd_kernel(qkv, keep, recv, acc_in, lse_in, side, out, k_s, v_s, kt_s, q_s, g_s, gt_s, dk_s, dv_s):
    mine = side[0] * HALF
    for b in range(HALF):
        gt_s[mine + b] = keep[b]
        gt_s[HALF - mine + b] = recv[b]
    rows_from(qkv, K, k_s)
    rows_from(qkv, V, v_s)
    rows_from(qkv, Q, q_s)
    rows_from(gt_s, ANY, g_s)
    wide_from(qkv, K, kt_s)
    dk_s[...] = jnp.zeros_like(dk_s)
    dv_s[...] = jnp.zeros_like(dv_s)

    def step(i, carry):
        g = cols(gt_s, i, ANY)
        delta = jnp.sum(g.astype(F32) * cols(acc_in, i, ANY), axis=0, keepdims=True)
        scores = nn(k_s[...], cols(qkv, i, Q))
        probs = jnp.exp2(scores * C2 - cols(lse_in, i, slice(0, 1)))
        gprobs = nn(v_s[...], g)
        ds = (probs * (gprobs - delta)).astype(BF16)
        put_cols(out, i, Q, nn(kt_s[...], ds) * FACTOR)
        at = pl.ds(pl.multiple_of(i * (QB * FB), QB * FB), QB * FB)
        dv_s[...] += nn(probs.astype(BF16), g_s[at, :])
        dk_s[...] += nn(ds, q_s[at, :])
        return carry

    lax.fori_loop(0, NB // QB, step, 0)
    for b in range(NB):
        part = slice(b * FB, (b + 1) * FB)
        out[b, K, :] = (dk_s[part, :] * FACTOR).T.astype(BF16)
        out[b, V, :] = dv_s[part, :].T.astype(BF16)


def backward(qkv, keep, recv, acc, lse):
    tall = pltpu.VMEM((FRAMES, HD), BF16)
    total = pltpu.VMEM((FRAMES, HD), F32)
    return call(
        bwd_kernel,
        [qkv, keep, recv, acc, lse],
        [shape((NB, 3 * HD, FB), BF16)],
        [
            tall,
            tall,
            pltpu.VMEM((HD, FRAMES), BF16),
            tall,
            tall,
            pltpu.VMEM((NB, HD, FB), BF16),
            total,
            total,
        ],
        side=True,
        us=16.2,
        name="bwd",
    )[0]


def weight_kernel(keep, recv, cot, w_pair, side, out, proj):
    low = side[0] == 0
    acc = jnp.zeros((PAIR, WIDTH), F32)
    for b in range(HALF):
        mine, other = keep[b], recv[b]
        rows = slice(b * FB, (b + 1) * FB)
        both = jnp.concatenate([jnp.where(low, mine, other), jnp.where(low, other, mine)], axis=0)
        acc = acc + nn(both, cot[rows, :])
        proj[rows, :] = nn(both.T, w_pair[...]).astype(BF16)
    out[...] = acc


def weight_part(keep, recv, cot, w_pair):
    return call(
        weight_kernel,
        [keep, recv, cot, w_pair],
        [shape((PAIR, WIDTH), F32), shape((HALF * FB, WIDTH), BF16)],
        side=True,
        us=6.4,
        name="grad_w",
    )


def weight_pairs():
    pairs = []
    for a in range(8):
        for n in range(32):
            b, s = divmod(n, 16)
            x, zl, zh = n // 8, n % 8 // 2, n % 2
            pairs.append(((a + 8 * b) * 16 + s, ((zl * 4 + x) * 2 + zh) * 8 + a))
    return pairs


def body(query, key_proj, value, cotangent, out_weight):
    flip = [(0, 1), (1, 0)]
    a2a = functools.partial(lax.all_to_all, split_axis=0, concat_axis=0, tiled=True)
    swap = lambda x: lax.ppermute(x, "zh", flip)
    after = lambda x, *others: lax.optimization_barrier((x, *others))[0]

    qkv = a2a(prep(query[0], key_proj[0], value[0]), SEQ)
    w_mine = lax.ppermute(after(out_weight, qkv), ALL, weight_pairs())
    cot = lax.all_gather(after(cotangent[0], qkv), YC, axis=0, tiled=True)
    att_keep, att_send, acc, lse = forward(qkv)
    w8 = a2a(after(jnp.broadcast_to(w_mine[None], (8, 6, WIDTH)), lse), Z8)
    att_recv = swap(att_send)
    w8 = after(w8, lse)
    w32 = a2a(jnp.broadcast_to(w8[None], (4, 8, 6, WIDTH)), "x").reshape(32, 6, WIDTH)
    w_pair, g_keep, g_send = grad_attended(w32, cot)
    g_recv = swap(after(g_send, att_recv))
    part, proj = weight_part(att_keep, att_recv, cot, w_pair)
    part = lax.psum_scatter(after(part, g_recv), "x", scatter_dimension=0, tiled=True)
    out = backward(qkv, g_keep, g_recv, acc, after(lse, proj))
    projected = lax.psum_scatter(after(proj, out), YC, scatter_dimension=0, tiled=True)
    grads = a2a(out, SEQ)
    parts = a2a(after(part, grads).astype(BF16).reshape(8, 6, WIDTH), Z8)
    grad_weight = jnp.sum(parts.astype(F32), axis=0)
    grad_weight = lax.ppermute(grad_weight, ALL, [(d, s) for s, d in weight_pairs()])

    grad_query, grad_key, grad_value = back(grads)
    return (projected[None], grad_query[None], grad_key[None], grad_value[None], grad_weight)


def solution(mesh):
    fine = Mesh(mesh.devices.reshape(4, 4, 2, 4, 2), ALL)
    rows = P(("zl", "x"), ("zh", "y", "c"), None)
    weight = P(ALL, None)
    return jax.shard_map(
        body,
        mesh=fine,
        in_specs=(rows, rows, rows, rows, weight),
        out_specs=(rows, rows, rows, rows, weight),
        check_vma=False,
    )
```

```python
import functools
import math

import jax
import jax.numpy as jnp
from jax import lax
from jax.experimental import pallas as pl
from jax.experimental.pallas import tpu as pltpu
from jax.sharding import Mesh
from jax.sharding import PartitionSpec as P

HD = 96
FACTOR = 1.0 / math.sqrt(HD)
LOG2E = math.log2(math.e)
C2 = FACTOR * LOG2E
F32 = jnp.float32
BF16 = jnp.bfloat16
NB = 16
HALF = 8
FB = 128
QB = 8
FRAMES = NB * FB
PAIR = 2 * HD
WIDTH = NB * HD
ALL = ("zl", "x", "zh", "y", "c")
SEQ = ("zh", "y", "c")
YC = ("y", "c")
Z8 = ("zl", "zh")


def call(kernel, ins, outs, scratch=(), side=False, us=1, name=None):
    vmem = pl.BlockSpec(memory_space=pltpu.VMEM)
    specs = [vmem for _ in ins]
    if side:
        ins = list(ins) + [lax.axis_index("zh").astype(jnp.int32).reshape(1)]
        specs.append(pl.BlockSpec(memory_space=pltpu.SMEM))
    return pl.pallas_call(
        kernel,
        out_shape=tuple(outs),
        in_specs=specs,
        out_specs=tuple(vmem for _ in outs),
        scratch_shapes=list(scratch),
        cost_estimate=pl.CostEstimate(flops=1, bytes_accessed=1, transcendentals=0),
        compiler_params=pltpu.CompilerParams(vmem_limit_bytes=56 * 2**20),
        name=name,
    )(*ins)


def shape(dims, dtype):
    return jax.ShapeDtypeStruct(dims, dtype)


def nn(a, b):
    return jnp.dot(a, b, preferred_element_type=F32)


Q, K, V = (slice(n * HD, (n + 1) * HD) for n in range(3))
ANY = slice(0, HD)


def cols(ref, step, rows):
    return jnp.concatenate([ref[step * QB + t, rows, :] for t in range(QB)], axis=1)


def put_cols(ref, step, rows, value):
    for t in range(QB):
        ref[step * QB + t, rows, :] = value[:, t * FB : (t + 1) * FB].astype(ref.dtype)


def rows_from(ref, rows, out):
    for b in range(NB):
        out[b * FB : (b + 1) * FB, :] = ref[b, rows, :].T


def wide_from(ref, rows, out):
    for b in range(NB):
        out[:, b * FB : (b + 1) * FB] = ref[b, rows, :]


def prep_kernel(q, k, v, out):
    for n, ref in enumerate((q, k, v)):
        for part in range(4):
            four = ref[:, part * 4 * HD : (part + 1) * 4 * HD].T
            for h in range(4):
                out[part * 4 + h, n * HD : (n + 1) * HD, :] = four[h * HD : (h + 1) * HD, :]


def prep(q, k, v):
    return call(prep_kernel, [q, k, v], [shape((NB, 3 * HD, FB), BF16)], us=2.6, name="prep")[0]


def back_kernel(src, *outs):
    for n, out in enumerate(outs):
        for part in range(4):
            four = [src[part * 4 + h, n * HD : (n + 1) * HD, :] for h in range(4)]
            out[:, part * 4 * HD : (part + 1) * 4 * HD] = jnp.concatenate(four, axis=0).T


def back(src):
    return call(back_kernel, [src], [shape((FB, WIDTH), BF16)] * 3, us=2.4, name="back")


def fwd_kernel(qkv, side, keep, send, acc_out, lse_out, k_s, vt_s, att):
    rows_from(qkv, K, k_s)
    wide_from(qkv, V, vt_s)
    lse_out[...] = jnp.zeros_like(lse_out)

    def step(i, carry):
        scores = nn(k_s[...], cols(qkv, i, Q))
        top = jnp.max(scores, axis=0, keepdims=True) * C2
        probs = jnp.exp2(scores * C2 - top)
        total = jnp.sum(probs, axis=0, keepdims=True)
        acc = nn(vt_s[...], probs.astype(BF16)) / total
        put_cols(att, i, ANY, acc)
        put_cols(acc_out, i, ANY, acc)
        put_cols(lse_out, i, slice(0, 1), top + jnp.log2(total))
        return carry

    lax.fori_loop(0, NB // QB, step, 0)
    mine = side[0] * HALF
    for b in range(HALF):
        keep[b] = att[mine + b]
        send[b] = att[HALF - mine + b]


def forward(qkv):
    half = shape((HALF, HD, FB), BF16)
    return call(
        fwd_kernel,
        [qkv],
        [half, half, shape((NB, HD, FB), F32), shape((NB, 8, FB), F32)],
        [
            pltpu.VMEM((FRAMES, HD), BF16),
            pltpu.VMEM((HD, FRAMES), BF16),
            pltpu.VMEM((NB, HD, FB), BF16),
        ],
        side=True,
        us=12.4,
        name="fwd",
    )


def grad_kernel(w32, cot, side, w_out, keep, send, w_s):
    for n in range(32):
        w_s[n * 6 : (n + 1) * 6, :] = w32[n].astype(F32)
    w_pair = w_s[...].astype(BF16)
    w_out[...] = w_pair
    low = side[0] == 0
    for b in range(HALF):
        both = lax.dot_general(
            w_pair, cot[b * FB : (b + 1) * FB, :], (((1,), (1,)), ((), ())), preferred_element_type=F32
        )
        keep[b] = jnp.where(low, both[:HD], both[HD:]).astype(BF16)
        send[b] = jnp.where(low, both[HD:], both[:HD]).astype(BF16)


def grad_attended(w32, cot):
    half = shape((HALF, HD, FB), BF16)
    return call(
        grad_kernel,
        [w32, cot],
        [shape((PAIR, WIDTH), BF16), half, half],
        [pltpu.VMEM((PAIR, WIDTH), F32)],
        side=True,
        us=4.4,
        name="grad_att",
    )


def bwd_kernel(qkv, keep, recv, acc_in, lse_in, side, out, k_s, v_s, kt_s, q_s, g_s, gt_s, dk_s, dv_s):
    mine = side[0] * HALF
    for b in range(HALF):
        gt_s[mine + b] = keep[b]
        gt_s[HALF - mine + b] = recv[b]
    rows_from(qkv, K, k_s)
    rows_from(qkv, V, v_s)
    rows_from(qkv, Q, q_s)
    rows_from(gt_s, ANY, g_s)
    wide_from(qkv, K, kt_s)
    dk_s[...] = jnp.zeros_like(dk_s)
    dv_s[...] = jnp.zeros_like(dv_s)

    def step(i, carry):
        g = cols(gt_s, i, ANY)
        delta = jnp.sum(g.astype(F32) * cols(acc_in, i, ANY), axis=0, keepdims=True)
        scores = nn(k_s[...], cols(qkv, i, Q))
        probs = jnp.exp2(scores * C2 - cols(lse_in, i, slice(0, 1)))
        gprobs = nn(v_s[...], g)
        ds = (probs * (gprobs - delta)).astype(BF16)
        put_cols(out, i, Q, nn(kt_s[...], ds) * FACTOR)
        at = pl.ds(pl.multiple_of(i * (QB * FB), QB * FB), QB * FB)
        dv_s[...] += nn(probs.astype(BF16), g_s[at, :])
        dk_s[...] += nn(ds, q_s[at, :])
        return carry

    lax.fori_loop(0, NB // QB, step, 0)
    for b in range(NB):
        part = slice(b * FB, (b + 1) * FB)
        out[b, K, :] = (dk_s[part, :] * FACTOR).T.astype(BF16)
        out[b, V, :] = dv_s[part, :].T.astype(BF16)


def backward(qkv, keep, recv, acc, lse):
    tall = pltpu.VMEM((FRAMES, HD), BF16)
    total = pltpu.VMEM((FRAMES, HD), F32)
    return call(
        bwd_kernel,
        [qkv, keep, recv, acc, lse],
        [shape((NB, 3 * HD, FB), BF16)],
        [
            tall,
            tall,
            pltpu.VMEM((HD, FRAMES), BF16),
            tall,
            tall,
            pltpu.VMEM((NB, HD, FB), BF16),
            total,
            total,
        ],
        side=True,
        us=16.2,
        name="bwd",
    )[0]


def weight_kernel(keep, recv, cot, w_pair, side, out, proj):
    low = side[0] == 0
    acc = jnp.zeros((PAIR, WIDTH), F32)
    for b in range(HALF):
        mine, other = keep[b], recv[b]
        rows = slice(b * FB, (b + 1) * FB)
        both = jnp.concatenate([jnp.where(low, mine, other), jnp.where(low, other, mine)], axis=0)
        acc = acc + nn(both, cot[rows, :])
        proj[rows, :] = nn(both.T, w_pair[...]).astype(BF16)
    out[...] = acc


def weight_part(keep, recv, cot, w_pair):
    return call(
        weight_kernel,
        [keep, recv, cot, w_pair],
        [shape((PAIR, WIDTH), F32), shape((HALF * FB, WIDTH), BF16)],
        side=True,
        us=6.4,
        name="grad_w",
    )


def weight_pairs():
    pairs = []
    for a in range(8):
        for n in range(32):
            b, s = divmod(n, 16)
            x, zl, zh = n // 8, n % 8 // 2, n % 2
            pairs.append(((a + 8 * b) * 16 + s, ((zl * 4 + x) * 2 + zh) * 8 + a))
    return pairs


def owner_pairs():
    pairs = []
    for a in range(8):
        for x in range(4):
            for z in range(8):
                src = (((z // 2) * 4 + x) * 2 + z % 2) * 8 + a
                pairs.append((src, ((a + 8 * (x // 2)) * 2 + x % 2) * 8 + z))
    return pairs


def body(query, key_proj, value, cotangent, out_weight):
    flip = [(0, 1), (1, 0)]
    a2a = functools.partial(lax.all_to_all, split_axis=0, concat_axis=0, tiled=True)
    swap = lambda x: lax.ppermute(x, "zh", flip)
    after = lambda x, *others: lax.optimization_barrier((x, *others))[0]

    qkv = a2a(prep(query[0], key_proj[0], value[0]), SEQ)
    w_mine = lax.ppermute(after(out_weight, qkv), ALL, weight_pairs())
    cot = lax.all_gather(after(cotangent[0], qkv), YC, axis=0, tiled=True)
    att_keep, att_send, acc, lse = forward(qkv)
    w8 = a2a(after(jnp.broadcast_to(w_mine[None], (8, 6, WIDTH)), lse), Z8)
    att_recv = swap(att_send)
    w8 = after(w8, lse)
    w32 = a2a(jnp.broadcast_to(w8[None], (4, 8, 6, WIDTH)), "x").reshape(32, 6, WIDTH)
    w_pair, g_keep, g_send = grad_attended(w32, cot)
    g_recv = swap(after(g_send, att_recv))
    part, proj = weight_part(att_keep, att_recv, cot, w_pair)
    part = lax.psum_scatter(after(part, g_recv), "x", scatter_dimension=0, tiled=True)
    out = backward(qkv, g_keep, g_recv, acc, after(lse, proj))
    projected = lax.psum_scatter(after(proj, out), YC, scatter_dimension=0, tiled=True)
    grads = a2a(out, SEQ)
    part = lax.ppermute(part.astype(BF16), ALL, owner_pairs())
    parts = a2a(after(part, grads).reshape(8, 6, WIDTH), YC)
    grad_weight = jnp.sum(parts.astype(F32), axis=0)

    grad_query, grad_key, grad_value = back(grads)
    return (projected[None], grad_query[None], grad_key[None], grad_value[None], grad_weight)


def solution(mesh):
    fine = Mesh(mesh.devices.reshape(4, 4, 2, 4, 2), ALL)
    rows = P(("zl", "x"), ("zh", "y", "c"), None)
    weight = P(ALL, None)
    return jax.shard_map(
        body,
        mesh=fine,
        in_specs=(rows, rows, rows, rows, weight),
        out_specs=(rows, rows, rows, rows, weight),
        check_vma=False,
    )
```

```python
import functools
import math

import jax
import jax.numpy as jnp
from jax import lax
from jax.experimental import pallas as pl
from jax.experimental.pallas import tpu as pltpu
from jax.sharding import Mesh
from jax.sharding import PartitionSpec as P

HD = 96
FACTOR = 1.0 / math.sqrt(HD)
LOG2E = math.log2(math.e)
C2 = FACTOR * LOG2E
F32 = jnp.float32
BF16 = jnp.bfloat16
NB = 16
HALF = 8
FB = 128
QB = 8
FRAMES = NB * FB
PAIR = 2 * HD
WIDTH = NB * HD
ALL = ("zl", "x", "zh", "y", "c")
SEQ = ("zh", "y", "c")
YC = ("y", "c")


def call(kernel, ins, outs, scratch=(), side=False, us=1, name=None):
    vmem = pl.BlockSpec(memory_space=pltpu.VMEM)
    specs = [vmem for _ in ins]
    if side:
        ins = list(ins) + [lax.axis_index("zh").astype(jnp.int32).reshape(1)]
        specs.append(pl.BlockSpec(memory_space=pltpu.SMEM))
    return pl.pallas_call(
        kernel,
        out_shape=tuple(outs),
        in_specs=specs,
        out_specs=tuple(vmem for _ in outs),
        scratch_shapes=list(scratch),
        cost_estimate=pl.CostEstimate(flops=1, bytes_accessed=1, transcendentals=0),
        compiler_params=pltpu.CompilerParams(vmem_limit_bytes=56 * 2**20),
        name=name,
    )(*ins)


def shape(dims, dtype):
    return jax.ShapeDtypeStruct(dims, dtype)


def nn(a, b):
    return jnp.dot(a, b, preferred_element_type=F32)


Q, K, V = (slice(n * HD, (n + 1) * HD) for n in range(3))
ANY = slice(0, HD)


def cols(ref, step, rows):
    return jnp.concatenate([ref[step * QB + t, rows, :] for t in range(QB)], axis=1)


def put_cols(ref, step, rows, value):
    for t in range(QB):
        ref[step * QB + t, rows, :] = value[:, t * FB : (t + 1) * FB].astype(ref.dtype)


def rows_from(ref, rows, out):
    for b in range(NB):
        out[b * FB : (b + 1) * FB, :] = ref[b, rows, :].T


def wide_from(ref, rows, out):
    for b in range(NB):
        out[:, b * FB : (b + 1) * FB] = ref[b, rows, :]


def prep_kernel(q, k, v, out):
    for n, ref in enumerate((q, k, v)):
        for part in range(4):
            four = ref[:, part * 4 * HD : (part + 1) * 4 * HD].T
            for h in range(4):
                out[part * 4 + h, n * HD : (n + 1) * HD, :] = four[h * HD : (h + 1) * HD, :]


def prep(q, k, v):
    return call(prep_kernel, [q, k, v], [shape((NB, 3 * HD, FB), BF16)], us=2.6, name="prep")[0]


def back_kernel(src, *outs):
    for n, out in enumerate(outs):
        for part in range(4):
            four = [src[part * 4 + h, n * HD : (n + 1) * HD, :] for h in range(4)]
            out[:, part * 4 * HD : (part + 1) * 4 * HD] = jnp.concatenate(four, axis=0).T


def back(src):
    return call(back_kernel, [src], [shape((FB, WIDTH), BF16)] * 3, us=2.4, name="back")


def fwd_kernel(qkv, side, keep, send, acc_out, lse_out, k_s, vt_s, att):
    rows_from(qkv, K, k_s)
    wide_from(qkv, V, vt_s)
    lse_out[...] = jnp.zeros_like(lse_out)

    def step(i, carry):
        scores = nn(k_s[...], cols(qkv, i, Q))
        top = jnp.max(scores, axis=0, keepdims=True) * C2
        probs = jnp.exp2(scores * C2 - top)
        total = jnp.sum(probs, axis=0, keepdims=True)
        acc = nn(vt_s[...], probs.astype(BF16)) / total
        put_cols(att, i, ANY, acc)
        put_cols(acc_out, i, ANY, acc)
        put_cols(lse_out, i, slice(0, 1), top + jnp.log2(total))
        return carry

    lax.fori_loop(0, NB // QB, step, 0)
    mine = side[0] * HALF
    for b in range(HALF):
        keep[b] = att[mine + b]
        send[b] = att[HALF - mine + b]


def forward(qkv):
    half = shape((HALF, HD, FB), BF16)
    return call(
        fwd_kernel,
        [qkv],
        [half, half, shape((NB, HD, FB), F32), shape((NB, 8, FB), F32)],
        [
            pltpu.VMEM((FRAMES, HD), BF16),
            pltpu.VMEM((HD, FRAMES), BF16),
            pltpu.VMEM((NB, HD, FB), BF16),
        ],
        side=True,
        us=12.4,
        name="fwd",
    )


def grad_kernel(w32, cot, side, w_out, keep, send, w_s):
    for n in range(32):
        w_s[n * 6 : (n + 1) * 6, :] = w32[n].astype(F32)
    w_pair = w_s[...].astype(BF16)
    w_out[...] = w_pair
    low = side[0] == 0
    for b in range(HALF):
        both = lax.dot_general(
            w_pair, cot[b * FB : (b + 1) * FB, :], (((1,), (1,)), ((), ())), preferred_element_type=F32
        )
        keep[b] = jnp.where(low, both[:HD], both[HD:]).astype(BF16)
        send[b] = jnp.where(low, both[HD:], both[:HD]).astype(BF16)


def grad_attended(w32, cot):
    half = shape((HALF, HD, FB), BF16)
    return call(
        grad_kernel,
        [w32, cot],
        [shape((PAIR, WIDTH), BF16), half, half],
        [pltpu.VMEM((PAIR, WIDTH), F32)],
        side=True,
        us=4.4,
        name="grad_att",
    )


def bwd_kernel(qkv, keep, recv, acc_in, lse_in, side, out, k_s, v_s, kt_s, q_s, g_s, gt_s, dk_s, dv_s):
    mine = side[0] * HALF
    for b in range(HALF):
        gt_s[mine + b] = keep[b]
        gt_s[HALF - mine + b] = recv[b]
    rows_from(qkv, K, k_s)
    rows_from(qkv, V, v_s)
    rows_from(qkv, Q, q_s)
    rows_from(gt_s, ANY, g_s)
    wide_from(qkv, K, kt_s)
    dk_s[...] = jnp.zeros_like(dk_s)
    dv_s[...] = jnp.zeros_like(dv_s)

    def step(i, carry):
        g = cols(gt_s, i, ANY)
        delta = jnp.sum(g.astype(F32) * cols(acc_in, i, ANY), axis=0, keepdims=True)
        scores = nn(k_s[...], cols(qkv, i, Q))
        probs = jnp.exp2(scores * C2 - cols(lse_in, i, slice(0, 1)))
        gprobs = nn(v_s[...], g)
        ds = (probs * (gprobs - delta)).astype(BF16)
        put_cols(out, i, Q, nn(kt_s[...], ds) * FACTOR)
        at = pl.ds(pl.multiple_of(i * (QB * FB), QB * FB), QB * FB)
        dv_s[...] += nn(probs.astype(BF16), g_s[at, :])
        dk_s[...] += nn(ds, q_s[at, :])
        return carry

    lax.fori_loop(0, NB // QB, step, 0)
    for b in range(NB):
        part = slice(b * FB, (b + 1) * FB)
        out[b, K, :] = (dk_s[part, :] * FACTOR).T.astype(BF16)
        out[b, V, :] = dv_s[part, :].T.astype(BF16)


def backward(qkv, keep, recv, acc, lse):
    tall = pltpu.VMEM((FRAMES, HD), BF16)
    total = pltpu.VMEM((FRAMES, HD), F32)
    return call(
        bwd_kernel,
        [qkv, keep, recv, acc, lse],
        [shape((NB, 3 * HD, FB), BF16)],
        [
            tall,
            tall,
            pltpu.VMEM((HD, FRAMES), BF16),
            tall,
            tall,
            pltpu.VMEM((NB, HD, FB), BF16),
            total,
            total,
        ],
        side=True,
        us=16.2,
        name="bwd",
    )[0]


def weight_kernel(keep, recv, cot, w_pair, side, out, proj):
    low = side[0] == 0
    acc = jnp.zeros((PAIR, WIDTH), F32)
    for b in range(HALF):
        mine, other = keep[b], recv[b]
        rows = slice(b * FB, (b + 1) * FB)
        both = jnp.concatenate([jnp.where(low, mine, other), jnp.where(low, other, mine)], axis=0)
        acc = acc + nn(both, cot[rows, :])
        proj[rows, :] = nn(both.T, w_pair[...]).astype(BF16)
    out[...] = acc


def weight_part(keep, recv, cot, w_pair):
    return call(
        weight_kernel,
        [keep, recv, cot, w_pair],
        [shape((PAIR, WIDTH), F32), shape((HALF * FB, WIDTH), BF16)],
        side=True,
        us=6.4,
        name="grad_w",
    )


def owner_pairs():
    pairs = []
    for a in range(8):
        for x in range(4):
            for z in range(8):
                src = (((z // 2) * 4 + x) * 2 + z % 2) * 8 + a
                pairs.append((src, ((a + 8 * (x // 2)) * 2 + x % 2) * 8 + z))
    return pairs


def body(query, key_proj, value, cotangent, out_weight):
    flip = [(0, 1), (1, 0)]
    a2a = functools.partial(lax.all_to_all, split_axis=0, concat_axis=0, tiled=True)
    swap = lambda x: lax.ppermute(x, "zh", flip)
    after = lambda x, *others: lax.optimization_barrier((x, *others))[0]

    w8 = a2a(jnp.broadcast_to(out_weight[None], (8, 6, WIDTH)), YC)
    qkv = a2a(after(prep(query[0], key_proj[0], value[0]), w8), SEQ)
    w8 = lax.ppermute(after(w8, qkv), ALL, [(d, s) for s, d in owner_pairs()])
    cot = lax.all_gather(after(cotangent[0], qkv), YC, axis=0, tiled=True)
    att_keep, att_send, acc, lse = forward(qkv)
    att_recv = swap(att_send)
    w8 = after(w8, lse)
    w32 = a2a(jnp.broadcast_to(w8[None], (4, 8, 6, WIDTH)), "x").reshape(32, 6, WIDTH)
    w_pair, g_keep, g_send = grad_attended(w32, cot)
    g_recv = swap(after(g_send, att_recv))
    part, proj = weight_part(att_keep, att_recv, cot, w_pair)
    part = lax.psum_scatter(after(part, g_recv), "x", scatter_dimension=0, tiled=True)
    out = backward(qkv, g_keep, g_recv, acc, after(lse, proj))
    projected = lax.psum_scatter(after(proj, out), YC, scatter_dimension=0, tiled=True)
    grads = a2a(out, SEQ)
    part = lax.ppermute(part.astype(BF16), ALL, owner_pairs())
    parts = a2a(after(part, grads).reshape(8, 6, WIDTH), YC)
    grad_weight = jnp.sum(parts.astype(F32), axis=0)

    grad_query, grad_key, grad_value = back(grads)
    return (projected[None], grad_query[None], grad_key[None], grad_value[None], grad_weight)


def solution(mesh):
    fine = Mesh(mesh.devices.reshape(4, 4, 2, 4, 2), ALL)
    rows = P(("zl", "x"), ("zh", "y", "c"), None)
    weight = P(ALL, None)
    return jax.shard_map(
        body,
        mesh=fine,
        in_specs=(rows, rows, rows, rows, weight),
        out_specs=(rows, rows, rows, rows, weight),
        check_vma=False,
    )
```
